256 devices in a mesh: gossip: 64 (over y_hi, z, x), fsdp: 4 (over y_lo, core).
Axes of the slice: x: 4, y: 4 (y_hi: 2, y_lo: 2; y = y_hi * 2 + y_lo), z: 8, core: 2. Of those that a mesh axis runs over, the one named last changes fastest.
Arguments:
- numerator: float32 [64, 2048, 2048], P('gossip', 'fsdp'), may hold values from -6 to 6
- push_weight: bfloat16 [64], P('gossip'), may hold values from 0.5 to 2
- hidden_in: bfloat16 [2, 64, 1024, 2048], P(None, 'gossip', 'fsdp'), may hold values from -6 to 6
- targets: bfloat16 [2, 64, 1024, 2048], P(None, 'gossip', 'fsdp'), may hold values from -6 to 6
- exponents: int32 [2], replicated, may hold values from 0 to 2
Outputs:
- params_out: float32 [64, 2048, 2048], P('gossip', 'fsdp')
- weight_out: float32 [64], P('gossip')
The draws below stay inside these ranges and needn't reach their ends.
Inputs may be any that keep to these rules, and one draw needn't show every extreme that they name: The push of step t goes 2**exponents[t] replicas further along, wrapping around.
All inputs are finite; a program needn't handle non-finite values.
Results may differ from the reference program's by a relative error of at most 0.014.
Values may be sent and summed in bfloat16 or wider, within the bound.
No kernel may reach another device: no remote copies, remote signals or barrier semaphores. Data moves between devices by JAX's collectives and lax.ppermute only.
A program may use at most 128 MiB of HBM per device.

```python
import math
import jax
import jax.numpy as jnp
from jax import lax

DW = 2048
HW = 2048
STEPS = 2
EXPONENTS = 3
TOK_DEV = 256
TOKENS_REP = 1024
REPLICAS = 64
N_GOSSIP = 64
N_FSDP = 4


def block_scale(key, dims, pieces, smallest, largest):
    def one(axis_at, blocks):
        steps = jax.random.uniform(jax.random.fold_in(jax.random.fold_in(key, 6), axis_at), (blocks,), jnp.float32, smallest / len(pieces), largest / len(pieces))
        return jnp.repeat(jnp.exp(steps), dims[axis_at] // blocks).reshape((-1,) + (1,) * (len(dims) - axis_at - 1))

    factor_of = one(*pieces[0])
    for cut in pieces[1:]:
        factor_of = factor_of * one(*cut)
    return factor_of


def bell_draw(rng, extent, spread, limit, pieces=(), kind=jnp.bfloat16):
    level = block_scale(rng, extent, pieces, -0.22, 0.18) if pieces else 1.0
    entries = jax.random.normal(rng, extent, jnp.float32) * spread * level
    return jnp.minimum(jnp.maximum(entries, -limit), limit).astype(kind)


def setup_inputs(seed: int = 0) -> dict:
    key_of = jax.random.split(jax.random.key(seed), 6)
    return {
        "numerator": bell_draw(key_of[0], (REPLICAS, HW, DW), 1.0, 6.0, ((0, 64), (1, 4)), jnp.float32),
        "push_weight": jnp.clip(jnp.exp(math.log(2.0) - 1.3862944 * jax.random.uniform(key_of[1], (REPLICAS,), jnp.float32) ** block_scale(key_of[1], (REPLICAS,), ((0, 64),), -0.2, 0.2)), 0.5, 2.0).astype(jnp.bfloat16),
        "hidden_in": bell_draw(key_of[2], (STEPS, REPLICAS, TOKENS_REP, DW), 1.0, 6.0, ((1, 64), (2, 4))),
        "targets": bell_draw(key_of[3], (STEPS, REPLICAS, TOKENS_REP, HW), 1.0, 6.0, ((1, 64), (2, 4))),
        "exponents": jax.random.randint(key_of[4], (STEPS,), 0, EXPONENTS).astype(jnp.int32),
    }


learning_rate = 0.5
epsilon = 1e-06

def normalize(hidden):
    values = hidden.astype(jnp.float32)
    scaled = values * lax.rsqrt(lax.optimization_barrier(jnp.mean(values * values, axis=-1, keepdims=True)) + epsilon)
    return scaled.astype(jnp.bfloat16)

def residual_term(preact, goal):
    sigma = jax.nn.sigmoid(preact)
    slope = sigma * (1.0 + preact * (1.0 - sigma))
    return ((preact * sigma - goal.astype(jnp.float32)) * slope).astype(jnp.bfloat16)

def replica_gradient(operands):
    numerators, weight, hidden, goal = operands
    current = (numerators / weight).astype(jnp.bfloat16)
    normed = normalize(hidden)
    preact = jnp.dot(normed, current.T, preferred_element_type=jnp.float32) / math.sqrt(DW)
    delta = residual_term(preact, goal)
    delta_blocks = delta.reshape(N_FSDP, TOK_DEV, HW).astype(jnp.float32)
    normed_blocks = normed.reshape(N_FSDP, TOK_DEV, DW).astype(jnp.float32)
    partial_sums = jnp.einsum('btj,bti->bji', delta_blocks, normed_blocks).astype(jnp.bfloat16)
    return lax.optimization_barrier(jnp.sum(partial_sums, axis=0, dtype=jnp.float32)) / math.sqrt(DW)

def reference(numerator, push_weight, hidden_in, targets, exponents):
    numerators = numerator
    weight = push_weight.astype(jnp.float32)
    positions = jnp.arange(N_GOSSIP, dtype=jnp.int32)
    pending_rows = None
    pending_weight = None
    for step in range(STEPS):
        gradient = lax.map(replica_gradient, (numerators, weight, hidden_in[step], targets[step]))
        halved = (numerators - learning_rate * gradient) * 0.5
        sent_rows = halved.astype(jnp.bfloat16)
        sent_weight = (weight * 0.5).astype(jnp.bfloat16)
        distance = jnp.left_shift(jnp.int32(1), exponents[step].astype(jnp.int32))
        source = ((positions - distance) % N_GOSSIP).astype(jnp.int32)
        arrived_rows = sent_rows[source]
        arrived_weight = sent_weight[source]
        numerators = halved
        weight = weight * 0.5
        if step > 0:
            numerators = numerators + pending_rows.astype(jnp.float32)
            weight = weight + pending_weight.astype(jnp.float32)
        pending_rows = arrived_rows
        pending_weight = arrived_weight
    numerators = numerators + pending_rows.astype(jnp.float32)
    weight = weight + pending_weight.astype(jnp.float32)
    return (numerators / weight[:, None, None], weight)
```

```python
from functools import partial
import math

import jax
import jax.numpy as jnp
from jax import lax
from jax.experimental import pallas as pl
from jax.experimental.pallas import tpu as pltpu
from jax.sharding import PartitionSpec as P

EXPONENTS = 3
CHUNKS = 2

learning_rate = 0.5
epsilon = 1e-06

AXES = ("gossip", "fsdp")


def swap(block, bit):
    n = lax.axis_size("fsdp")
    return lax.ppermute(block, "fsdp", [(i, i ^ bit) for i in range(n)])


def pushed(block, distance):
    n = lax.axis_size("gossip")
    return lax.ppermute(block, "gossip", [(i, (i + distance) % n) for i in range(n)])


def row_scale(h):
    values = h.astype(jnp.float32)
    return lax.rsqrt(jnp.mean(values * values, axis=-1, keepdims=True) + epsilon)


def step_kernel(mix, f_ref, w_ref, h0, h1, h2, h3, t0, t1, t2, t3, n_ref, *rest):
    if mix == 1:
        halved_ref, scales = rest
    else:
        halved_ref, message_ref, scales = rest
    width = n_ref.shape[-1]
    root_width = math.sqrt(width)

    @pl.when(pl.program_id(0) == 0)
    def _():
        for b, h in enumerate((h0, h1, h2, h3)):
            scales[b] = row_scale(h[...].reshape(h.shape[-2:]))

    current = (n_ref[...] / w_ref[0]).astype(jnp.bfloat16)
    total = None
    for b, (h, t) in enumerate(((h0, t0), (h1, t1), (h2, t2), (h3, t3))):
        tokens = h[...].reshape(h.shape[-2:])
        goal = t[...].reshape(t.shape[-2:]).astype(jnp.float32)
        scale = scales[b]
        raw = lax.dot_general(
            tokens, current, (((1,), (1,)), ((), ())), preferred_element_type=jnp.float32
        )
        preact = raw * (scale * (1.0 / root_width))
        sigma = jax.nn.sigmoid(preact)
        slope = sigma * (1.0 + preact * (1.0 - sigma))
        delta = (((preact * sigma - goal) * slope) * scale).astype(jnp.bfloat16)
        part = lax.dot_general(
            delta, tokens, (((0,), (0,)), ((), ())), preferred_element_type=jnp.float32
        )
        total = part if total is None else total + part
    halved = (n_ref[...] - (learning_rate / root_width) * total) * 0.5
    halved_ref[...] = halved
    if mix == 0:
        message_ref[...] = halved.astype(jnp.bfloat16)
    elif mix == 2:
        message_ref[...] = (n_ref[...] + halved).astype(jnp.bfloat16)


def run_step(mix, step, f, weight, hs, ts, chunk, chunks, rows, offset):
    n_tok, width = hs[1].shape
    count = ts[3].shape[-1]
    sub = min(256, count)
    steps = count // sub
    first = chunk * steps
    total_steps = chunks * steps
    row_base = offset // sub
    in_specs = [
        pl.BlockSpec((1, 1, n_tok, width), lambda i, f, w: (step, 0, 0, 0)),
        pl.BlockSpec((n_tok, width), lambda i, f, w: (0, 0)),
        pl.BlockSpec((n_tok, width), lambda i, f, w: (0, 0)),
        pl.BlockSpec((n_tok, width), lambda i, f, w: (0, 0)),
        pl.BlockSpec((1, 1, n_tok, sub), lambda i, f, w: (step, 0, 0, f[0] * total_steps + first + i)),
        pl.BlockSpec((n_tok, sub), lambda i, f, w: (0, i)),
        pl.BlockSpec((n_tok, sub), lambda i, f, w: (0, first + i)),
        pl.BlockSpec((n_tok, sub), lambda i, f, w: (1, i)),
        pl.BlockSpec((sub, width), lambda i, f, w: (row_base + i, 0)),
    ]
    out_shape = [jax.ShapeDtypeStruct((count, width), jnp.float32)]
    out_specs = [pl.BlockSpec((sub, width), lambda i, f, w: (i, 0))]
    if mix != 1:
        out_shape.append(jax.ShapeDtypeStruct((count, width), jnp.bfloat16))
        out_specs.append(pl.BlockSpec((sub, width), lambda i, f, w: (i, 0)))
    return pl.pallas_call(
        partial(step_kernel, mix),
        grid_spec=pltpu.PrefetchScalarGridSpec(
            num_scalar_prefetch=2,
            grid=(steps,),
            in_specs=in_specs,
            out_specs=out_specs,
            scratch_shapes=[pltpu.VMEM((4, n_tok, 1), jnp.float32)],
        ),
        out_shape=out_shape,
        compiler_params=pltpu.CompilerParams(vmem_limit_bytes=48 * 2**20),
        cost_estimate=pl.CostEstimate(
            flops=16 * n_tok * width * count,
            bytes_accessed=8 * n_tok * width + 10 * count * width + 8 * n_tok * count,
            transcendentals=4 * n_tok * count,
        ),
        name="step_rows",
    )(f, weight, *hs, *ts, rows)


def whole(k0, k1, numerator, push_weight, hidden_in, targets):
    numerators = numerator[0]
    n_rows, width = numerators.shape
    n_tok = hidden_in.shape[2]
    count = n_rows // CHUNKS
    weight = push_weight.astype(jnp.float32)
    f = lax.axis_index("fsdp")
    f_arr = f.astype(jnp.int32)[None]
    same = k0 == k1
    d0, d1 = 1 << k0, 1 << k1

    def columns(step, owner, start, size):
        return lax.dynamic_slice(targets[step, 0], (0, owner * n_rows + start), (n_tok, size))

    hid_y, tgt_y = [], []
    for step in range(2):
        hid_y.append(swap(hidden_in[step, 0], 2))
        tgt_y.append([
            swap(
                jnp.concatenate(
                    [columns(step, f ^ 2, c * count, count), columns(step, f ^ 3, c * count, count)], axis=0
                ),
                2,
            )
            for c in range(CHUNKS)
        ])
    w0 = pushed((weight * 0.5).astype(jnp.bfloat16), d0).astype(jnp.float32)
    w1 = pushed((weight * 0.25).astype(jnp.bfloat16), d1).astype(jnp.float32)
    weight_out = (weight * 0.25 + w0) + w1

    hs, ts = [], []
    for step in range(2):
        hs.append([hidden_in, hid_y[step], swap(hidden_in[step, 0], 1), swap(hid_y[step], 1)])
        own_core = swap(columns(step, f ^ 1, 0, n_rows), 1)
        ts.append([
            [targets, tgt_y[step][c], own_core, swap(tgt_y[step][c], 1)] for c in range(CHUNKS)
        ])

    halved, arrived0 = [], []
    for c in range(CHUNKS):
        out = run_step(1 if same else 0, 0, f_arr, weight, hs[0], ts[0][c], c, CHUNKS, numerators, c * count)
        halved.append(out[0])
        if not same:
            arrived0.append(pushed(out[1], d0))
    pieces = []
    for c in range(CHUNKS):
        out = run_step(2 if same else 0, 1, f_arr, weight * 0.5, hs[1], ts[1][c], c, CHUNKS, halved[c], 0)
        total = out[0] + pushed(out[1], d1).astype(jnp.float32)
        if not same:
            total = total + arrived0[c].astype(jnp.float32)
        pieces.append(total / weight_out[0])
    return jnp.concatenate(pieces, axis=0)[None], weight_out


def per_device(numerator, push_weight, hidden_in, targets, exponents):
    branches = [partial(whole, k0, k1) for k0 in range(EXPONENTS) for k1 in range(EXPONENTS)]
    return lax.switch(
        exponents[0] * EXPONENTS + exponents[1], branches, numerator, push_weight, hidden_in, targets
    )


def solution(mesh):
    in_specs = (
        P("gossip", "fsdp", None),
        P("gossip"),
        P(None, "gossip", "fsdp", None),
        P(None, "gossip", "fsdp", None),
        P(),
    )
    out_specs = (P("gossip", "fsdp", None), P("gossip"))
    return jax.shard_map(
        per_device, mesh=mesh, in_specs=in_specs, out_specs=out_specs, check_vma=False
    )
```

```python
from functools import partial
import math

import jax
import jax.numpy as jnp
from jax import lax
from jax.experimental import pallas as pl
from jax.experimental.pallas import tpu as pltpu
from jax.sharding import PartitionSpec as P

EXPONENTS = 3
CHUNKS = 2
RING = 4
TILE = 512
VMEM = 63 * 2**20

learning_rate = 0.5
epsilon = 1e-06


def swap(block, bit):
    n = lax.axis_size("fsdp")
    return lax.ppermute(block, "fsdp", [(i, i ^ bit) for i in range(n)])


def pushed(block, distance):
    n = lax.axis_size("gossip")
    return lax.ppermute(block, "gossip", [(i, (i + distance) % n) for i in range(n)])


def after(block, *earlier):
    return lax.optimization_barrier((block, *earlier))[0]


def norm_kernel(h_ref, out_ref):
    values = h_ref[0, 0].astype(jnp.float32)
    scale = lax.rsqrt(jnp.mean(values * values, axis=-1, keepdims=True) + epsilon)
    out_ref[...] = (values * scale).astype(jnp.bfloat16)


def normalized(hidden_in, step):
    _, _, n_tok, width = hidden_in.shape
    tile = 128
    return pl.pallas_call(
        norm_kernel,
        grid=(n_tok // tile,),
        in_specs=[pl.BlockSpec((1, 1, tile, width), lambda i: (step, 0, i, 0))],
        out_specs=pl.BlockSpec((tile, width), lambda i: (i, 0)),
        out_shape=jax.ShapeDtypeStruct((n_tok, width), jnp.bfloat16),
        compiler_params=pltpu.CompilerParams(vmem_limit_bytes=VMEM),
        name="normalize",
    )(hidden_in)


def copy_kernel(f_ref, t_ref, out_ref):
    out_ref[0] = t_ref[0, 0]


def packed(f, targets, n_rows, owners):
    steps, _, n_tok, _ = targets.shape
    return pl.pallas_call(
        copy_kernel,
        grid_spec=pltpu.PrefetchScalarGridSpec(
            num_scalar_prefetch=1,
            grid=(steps, len(owners)),
            in_specs=[
                pl.BlockSpec(
                    (1, 1, n_tok, n_rows), lambda s, o, f: (s, 0, 0, jnp.bitwise_xor(f[0], owners[0] + o))
                )
            ],
            out_specs=pl.BlockSpec((1, n_tok, n_rows), lambda s, o, f: (s, o, 0)),
        ),
        out_shape=jax.ShapeDtypeStruct((steps, len(owners) * n_tok, n_rows), jnp.bfloat16),
        compiler_params=pltpu.CompilerParams(vmem_limit_bytes=VMEM),
        name="pack_targets",
    )(f, targets)


def pair_kernel(last, w_ref, same_ref, f_ref, left_ref, n0, n1, t0, t1, rows_ref, *refs, step):
    deltas = refs[-1]
    width = left_ref.shape[1]
    root_width = math.sqrt(width)
    n_tok = n0.shape[0]

    @pl.when(pl.program_id(0) == 0)
    def _():
        scale = 2.0**step / (root_width * w_ref[0])
        for b, (n, t) in enumerate(((n0, t0), (n1, t1))):
            pre = scale * lax.dot_general(
                n[...], left_ref[...], (((1,), (1,)), ((), ())), preferred_element_type=jnp.float32
            )
            goal = t[...].reshape(t.shape[-2:]).astype(jnp.float32)
            sigma = jax.nn.sigmoid(pre)
            slope = sigma * (1.0 + pre * (1.0 - sigma))
            deltas[:, b * n_tok : (b + 1) * n_tok] = ((pre * sigma - goal) * slope).astype(jnp.bfloat16).T

    k = pl.ds(pl.multiple_of(pl.program_id(0) * TILE, TILE), TILE)
    total = jnp.dot(deltas[:, :n_tok], n0[:, k], preferred_element_type=jnp.float32)
    total += jnp.dot(deltas[:, n_tok:], n1[:, k], preferred_element_type=jnp.float32)
    rows = rows_ref[...] - (learning_rate / root_width) * total
    if not last:
        refs[0][...] = rows
        return
    halved_ref, first_ref, second_ref = refs[:3]
    halved = rows * 0.5
    halved_ref[...] = halved
    message = halved
    if step == 1:
        message = jnp.where(same_ref[0] != 0, left_ref[:, k].astype(jnp.float32) + halved, halved)
    message = message.astype(jnp.bfloat16)
    half = first_ref.shape[0]
    first_ref[...] = message[:half]
    second_ref[...] = message[half:]


def pair(step, last, weight, same, f, left, ns, ts, rows):
    n_tok, width = ns[0].shape
    n_rows = rows.shape[0]
    half = n_rows // CHUNKS

    def goal(t, i):
        if i is None:
            return pl.BlockSpec((1, 1, n_tok, n_rows), lambda j, w, s, f: (step, 0, 0, f[0]))
        return pl.BlockSpec((1, n_tok, n_rows), lambda j, w, s, f: (step, i, 0))

    whole = pl.BlockSpec((n_rows, width), lambda j, w, s, f: (0, 0))
    tile = pl.BlockSpec((n_rows, TILE), lambda j, w, s, f: (0, j))
    out_specs = [tile]
    out_shape = [jax.ShapeDtypeStruct((n_rows, width), jnp.float32)]
    if last:
        out_specs += [pl.BlockSpec((half, TILE), lambda j, w, s, f: (0, j))] * 2
        out_shape += [jax.ShapeDtypeStruct((half, width), jnp.bfloat16)] * 2
    return pl.pallas_call(
        partial(pair_kernel, last, step=step),
        grid_spec=pltpu.PrefetchScalarGridSpec(
            num_scalar_prefetch=3,
            grid=(width // TILE,),
            in_specs=[whole]
            + [pl.BlockSpec((n_tok, width), lambda j, w, s, f: (0, 0))] * 2
            + [goal(*t) for t in ts]
            + [tile],
            out_specs=out_specs,
            scratch_shapes=[pltpu.VMEM((n_rows, 2 * n_tok), jnp.bfloat16)],
        ),
        out_shape=out_shape,
        compiler_params=pltpu.CompilerParams(vmem_limit_bytes=VMEM),
        cost_estimate=pl.CostEstimate(flops=2**20, bytes_accessed=2**20, transcendentals=0),
        name="pair_of_blocks",
    )(weight, same, f, left, *ns, *(t for t, _ in ts), rows)


def sum_kernel(w_ref, *refs):
    source, arrived = refs[0], [refs[1 + 2 * c : 3 + 2 * c] for c in range(CHUNKS)]
    out, halved, first, second, in_sems, out_sems = refs[1 + 2 * CHUNKS :]
    bufs = (halved, first, second)
    count = halved.shape[0] // CHUNKS
    pieces = in_sems.shape[2]
    piece = count // pieces
    factor = 1.0 / w_ref[0]

    def part(c, i):
        return pl.ds(pl.multiple_of(c * count + i * piece, piece), piece)

    def copies_in(c, i):
        there = pl.ds(pl.multiple_of(i * piece, piece), piece)
        froms = [source.at[part(c, i)]] + [a.at[there] for a in arrived[c]]
        return [
            pltpu.make_async_copy(x, bufs[a].at[part(c, i)], in_sems.at[c, a, i]) for a, x in enumerate(froms)
        ]

    def copy_out(c, i):
        return pltpu.make_async_copy(halved.at[part(c, i)], out.at[part(c, i)], out_sems.at[c, i])

    def run(c, body):
        lax.fori_loop(0, pieces, lambda i, _: (body(c, i), 0)[1], 0)

    def start(c, i):
        for x in copies_in(c, i):
            x.start()

    def work(c, i):
        for x in copies_in(c, i):
            x.wait()

        def strip(j, _):
            s = pl.ds(pl.multiple_of(c * count + i * piece + j * 16, 16), 16)
            halved[s] = (halved[s] + first[s].astype(jnp.float32) + second[s].astype(jnp.float32)) * factor
            return 0

        lax.fori_loop(0, piece // 16, strip, 0)
        copy_out(c, i).start()

    for c in range(CHUNKS):
        run(c, start)
    for c in range(CHUNKS):
        run(c, work)
    for c in range(CHUNKS):
        run(c, lambda c, i: copy_out(c, i).wait())


def divided(weight, halved, first, second):
    n_rows, width = halved.shape
    pieces = 4
    operands = [halved] + [x for chunk in zip(first, second) for x in chunk]
    anywhere = pl.BlockSpec(memory_space=pl.ANY)
    return pl.pallas_call(
        sum_kernel,
        grid_spec=pltpu.PrefetchScalarGridSpec(
            num_scalar_prefetch=1,
            grid=(),
            in_specs=[anywhere] * len(operands),
            out_specs=anywhere,
            scratch_shapes=[
                pltpu.VMEM((n_rows, width), jnp.float32),
                pltpu.VMEM((n_rows, width), jnp.bfloat16),
                pltpu.VMEM((n_rows, width), jnp.bfloat16),
                pltpu.SemaphoreType.DMA((CHUNKS, 3, pieces)),
                pltpu.SemaphoreType.DMA((CHUNKS, pieces)),
            ],
        ),
        out_shape=jax.ShapeDtypeStruct((n_rows, width), jnp.float32),
        compiler_params=pltpu.CompilerParams(vmem_limit_bytes=VMEM),
        name="last_sum",
    )(weight, *operands)


def along(block, distance):
    n = lax.axis_size("gossip")
    return lax.ppermute(block, "gossip", [(i, i - i % RING + (i + distance) % RING) for i in range(n)])


def across(block, wrapped):
    n = lax.axis_size("gossip")
    return lax.ppermute(block, "gossip", [(i, (i + RING) % n if i % RING in wrapped else i) for i in range(n)])


def exchange(k0, k1, m0, m1):
    if k0 == k1:
        return [jnp.zeros_like(m) for m in m0], [pushed(m, 1 << k1) for m in m1]
    begun = []
    for k, m in ((k0, m0), (k1, m1)):
        d = 1 << k
        if d < RING:
            begun.append([along(m[0], d), across(m[1], range(RING - d, RING))])
        else:
            begun.append([pushed(x, d) for x in m])
    sent = []
    for k, m in zip((k0, k1), begun):
        d = 1 << k
        sent.append([across(m[0], range(d)), along(m[1], d)] if d < RING else m)
    return sent[0], sent[1]


def per_device(numerator, push_weight, hidden_in, targets, exponents):
    numerators = numerator[0]
    n_rows, width = numerators.shape
    weight = push_weight.astype(jnp.float32)
    same = (exponents[0] == exponents[1]).astype(jnp.int32)[None]
    f = lax.axis_index("fsdp").astype(jnp.int32)[None]

    own0 = normalized(hidden_in, 0)
    chip0 = swap(own0, 2)
    t_chip_out = packed(f, targets, n_rows, (2, 3))
    t_chip = swap(t_chip_out, 2)
    own1 = normalized(after(hidden_in, t_chip_out), 1)
    chip1 = swap(own1, 2)

    t_core_out = packed(after(f, own1), targets, n_rows, (1,))
    received = []
    tile = jnp.broadcast_to(push_weight, (16, 128))
    for k in range(EXPONENTS):
        tile = after(tile, t_core_out, *received)
        received.append(pushed(tile, 1 << k))
    received = [x[0, :1].astype(jnp.float32) for x in received]

    def chosen(k):
        return jnp.where(k == 0, received[0], jnp.where(k == 1, received[1], received[2]))

    weight_out = (weight * 0.25 + chosen(exponents[0]) * 0.5) + chosen(exponents[1]) * 0.25

    current0 = after(numerators, own1).astype(jnp.bfloat16)
    chip0 = after(chip0, current0, weight_out)
    core0 = swap(after(own0, chip0), 1)
    core1 = swap(after(own1, chip0), 1)
    t_core = swap(after(t_core_out, chip0), 1)
    corner0 = swap(chip0, 1)
    t_corner = swap(t_chip, 1)
    t_near = [(targets, None), (t_core, 0)]
    t_far = [(t_chip, 0), (t_corner, 1)]
    [rows0] = pair(0, False, weight, same, f, current0, [own0, core0], t_near, numerators)
    halved0, *m0 = pair(0, True, weight, same, f, current0, [chip0, corner0], t_far, rows0)
    left1 = jnp.concatenate(m0, axis=0)
    [rows1] = pair(1, False, weight, same, f, left1, [own1, core1], t_near, halved0)
    chip1 = after(chip1, rows1)
    halved1, *m1 = pair(1, True, weight, same, f, left1, [chip1, swap(chip1, 1)], t_far, rows1)

    branches = [partial(exchange, k0, k1) for k0 in range(EXPONENTS) for k1 in range(EXPONENTS)]
    a0, a1 = lax.switch(exponents[0] * EXPONENTS + exponents[1], branches, m0, m1)
    return divided(weight_out, halved1, a0, a1)[None], weight_out


def solution(mesh):
    in_specs = (
        P("gossip", "fsdp", None),
        P("gossip"),
        P(None, "gossip", "fsdp", None),
        P(None, "gossip", "fsdp", None),
        P(),
    )
    out_specs = (P("gossip", "fsdp", None), P("gossip"))
    return jax.shard_map(
        per_device, mesh=mesh, in_specs=in_specs, out_specs=out_specs, check_vma=False
    )
```

```python
from functools import partial
import math

import jax
import jax.numpy as jnp
from jax import lax
from jax.experimental import pallas as pl
from jax.experimental.pallas import tpu as pltpu
from jax.sharding import PartitionSpec as P

EXPONENTS = 3
CHUNKS = 2
RING = 4
TILE = 1024
VMEM = 63 * 2**20

learning_rate = 0.5
epsilon = 1e-06


def swap(block, bit):
    n = lax.axis_size("fsdp")
    return lax.ppermute(block, "fsdp", [(i, i ^ bit) for i in range(n)])


def pushed(block, distance):
    n = lax.axis_size("gossip")
    return lax.ppermute(block, "gossip", [(i, (i + distance) % n) for i in range(n)])


def after(block, *earlier):
    return lax.optimization_barrier((block, *earlier))[0]


def norm(h):
    values = h.astype(jnp.float32)
    scale = lax.rsqrt(jnp.mean(values * values, axis=-1, keepdims=True) + epsilon)
    return (values * scale).astype(jnp.bfloat16)


def norm_kernel(h_ref, out_ref):
    out_ref[...] = norm(h_ref[0, 0])


def normalized(hidden_in, step):
    _, _, n_tok, width = hidden_in.shape
    tile = 128
    return pl.pallas_call(
        norm_kernel,
        grid=(n_tok // tile,),
        in_specs=[pl.BlockSpec((1, 1, tile, width), lambda i: (step, 0, i, 0))],
        out_specs=pl.BlockSpec((tile, width), lambda i: (i, 0)),
        out_shape=jax.ShapeDtypeStruct((n_tok, width), jnp.bfloat16),
        compiler_params=pltpu.CompilerParams(vmem_limit_bytes=VMEM),
        name="normalize",
    )(hidden_in)


def first_kernel(f_ref, h_ref, t0_ref, t1_ref, out_ref):
    step = pl.program_id(0)

    @pl.when(step == 0)
    def _():
        out_ref[...] = norm(h_ref[0, 0])

    @pl.when(step == 1)
    def _():
        half = out_ref.shape[1] // 2
        out_ref[:, :half] = t0_ref[0, 0]
        out_ref[:, half:] = t1_ref[0, 0]


def first_message(f, hidden_in, targets):
    _, _, n_tok, width = hidden_in.shape
    half = width // 2
    tile = 128
    per_step = n_tok // tile

    def of_step(step):
        return pl.BlockSpec(
            (1, 1, tile, half), lambda part, i, f: (step, 0, i * part, jnp.bitwise_xor(f[0] // 2, 1))
        )

    return pl.pallas_call(
        first_kernel,
        grid_spec=pltpu.PrefetchScalarGridSpec(
            num_scalar_prefetch=1,
            grid=(2, per_step),
            in_specs=[
                pl.BlockSpec((1, 1, tile, width), lambda part, i, f: (0, 0, i * (1 - part) + (per_step - 1) * part, 0)),
                of_step(0),
                of_step(1),
            ],
            out_specs=pl.BlockSpec((tile, width), lambda part, i, f: (part * per_step + i, 0)),
        ),
        out_shape=jax.ShapeDtypeStruct((2 * n_tok, width), jnp.bfloat16),
        compiler_params=pltpu.CompilerParams(vmem_limit_bytes=VMEM),
        name="first_message",
    )(f, hidden_in, targets, targets)


def copy_kernel(f_ref, t_ref, out_ref):
    out_ref[0] = t_ref[0, 0]


def for_other_core(f, targets, n_rows):
    steps, _, n_tok, _ = targets.shape
    return pl.pallas_call(
        copy_kernel,
        grid_spec=pltpu.PrefetchScalarGridSpec(
            num_scalar_prefetch=1,
            grid=(steps,),
            in_specs=[pl.BlockSpec((1, 1, n_tok, n_rows), lambda s, f: (s, 0, 0, jnp.bitwise_xor(f[0], 1)))],
            out_specs=pl.BlockSpec((1, n_tok, n_rows), lambda s, f: (s, 0, 0)),
        ),
        out_shape=jax.ShapeDtypeStruct((steps, n_tok, n_rows), jnp.bfloat16),
        compiler_params=pltpu.CompilerParams(vmem_limit_bytes=VMEM),
        name="pack_targets",
    )(f, targets)


def pair_kernel(last, w_ref, order_ref, f_ref, l0, l1, n0, n1, t0, t1, rows_ref, *refs, step):
    deltas = refs[-1]
    half, width = l0.shape
    root_width = math.sqrt(width)
    n_tok = n0.shape[0]

    @pl.when(pl.program_id(0) == 0)
    def _():
        scale = 2.0**step / (root_width * w_ref[0])
        for b, (n, t) in enumerate(((n0, t0), (n1, t1))):
            goals = t[...].reshape(t.shape[-2:])
            for c, left in enumerate((l0, l1)):
                pre = scale * lax.dot_general(
                    n[...], left[...], (((1,), (1,)), ((), ())), preferred_element_type=jnp.float32
                )
                goal = goals[:, c * half : (c + 1) * half].astype(jnp.float32)
                sigma = jax.nn.sigmoid(pre)
                slope = sigma * (1.0 + pre * (1.0 - sigma))
                delta = ((pre * sigma - goal) * slope).astype(jnp.bfloat16)
                deltas[c * half : (c + 1) * half, b * n_tok : (b + 1) * n_tok] = delta.T

    k = pl.ds(pl.multiple_of(pl.program_id(0) * TILE, TILE), TILE)
    total = jnp.dot(deltas[:, :n_tok], n0[:, k], preferred_element_type=jnp.float32)
    total += jnp.dot(deltas[:, n_tok:], n1[:, k], preferred_element_type=jnp.float32)
    rows = rows_ref[...] - (learning_rate / root_width) * total
    if not last:
        refs[0][...] = rows
        return
    halved = rows * 0.5
    refs[0][...] = halved
    for c, left in enumerate((l0, l1)):
        here = halved[c * half : (c + 1) * half]
        message = here.astype(jnp.bfloat16)
        if step == 0:
            refs[1 + c][...] = message
        else:
            earlier = left[:, k]
            both = (earlier.astype(jnp.float32) + here).astype(jnp.bfloat16)
            swapped = order_ref[0] > order_ref[1]
            near = jnp.where(swapped, message, earlier)
            refs[1 + c][...] = jnp.where(order_ref[0] == order_ref[1], both, near)
            refs[3 + c][...] = jnp.where(swapped, earlier, message)


def pair(step, last, weight, order, f, n_tok, left, ns, ts, rows):
    n_rows, width = rows.shape
    half = n_rows // CHUNKS

    def goal(t):
        if t.ndim == 4:
            return pl.BlockSpec((1, 1, n_tok, n_rows), lambda j, w, s, f: (step, 0, 0, f[0]))
        if t.ndim == 3:
            return pl.BlockSpec((1, n_tok, n_rows), lambda j, w, s, f: (step, 0, 0))
        return pl.BlockSpec((n_tok, n_rows), lambda j, w, s, f: (1, step * 2 + f[0] % 2))

    if len(left) == 1:
        left = [left[0], left[0]]
        halves = [pl.BlockSpec((half, width), lambda j, w, s, f, c=c: (c, 0)) for c in range(CHUNKS)]
    else:
        halves = [pl.BlockSpec((half, width), lambda j, w, s, f: (0, 0))] * CHUNKS
    tile = pl.BlockSpec((n_rows, TILE), lambda j, w, s, f: (0, j))
    out_specs = [tile]
    out_shape = [jax.ShapeDtypeStruct((n_rows, width), jnp.float32)]
    if last:
        out_specs += [pl.BlockSpec((half, TILE), lambda j, w, s, f: (0, j))] * (2 + 2 * step)
        out_shape += [jax.ShapeDtypeStruct((half, width), jnp.bfloat16)] * (2 + 2 * step)
    return pl.pallas_call(
        partial(pair_kernel, last, step=step),
        grid_spec=pltpu.PrefetchScalarGridSpec(
            num_scalar_prefetch=3,
            grid=(width // TILE,),
            in_specs=halves
            + [pl.BlockSpec((n_tok, width), lambda j, w, s, f: (0, 0))] * 2
            + [goal(t) for t in ts]
            + [tile],
            out_specs=out_specs,
            scratch_shapes=[pltpu.VMEM((n_rows, 2 * n_tok), jnp.bfloat16)],
        ),
        out_shape=out_shape,
        compiler_params=pltpu.CompilerParams(vmem_limit_bytes=VMEM),
        cost_estimate=pl.CostEstimate(flops=2**20, bytes_accessed=2**20, transcendentals=0),
        name="pair_of_blocks",
    )(weight, order, f, *left, *ns, *ts, rows)


def sum_kernel(chunks, n_arrived, w_ref, *refs):
    source, arrived = refs[0], refs[1 : 1 + len(chunks) * n_arrived]
    out = refs[-(n_arrived + 4)]
    bufs, (in_sems, out_sems) = refs[-(n_arrived + 3) : -2], refs[-2:]
    pieces = in_sems.shape[2]
    count = bufs[0].shape[0] // len(chunks)
    piece = count // pieces
    factor = 1.0 / w_ref[0]

    def rows(at, i):
        return pl.ds(pl.multiple_of(at * count + i * piece, piece), piece)

    def copies_in(c, i):
        froms = [source.at[rows(chunks[c], i)]]
        froms += [a.at[rows(0, i)] for a in arrived[c * n_arrived : (c + 1) * n_arrived]]
        return [
            pltpu.make_async_copy(x, bufs[a].at[rows(c, i)], in_sems.at[c, a, i]) for a, x in enumerate(froms)
        ]

    def copy_out(c, i):
        return pltpu.make_async_copy(bufs[0].at[rows(c, i)], out.at[rows(chunks[c], i)], out_sems.at[c, i])

    def run(c, body):
        lax.fori_loop(0, pieces, lambda i, _: (body(c, i), 0)[1], 0)

    def start(c, i):
        for x in copies_in(c, i):
            x.start()

    def work(c, i):
        for x in copies_in(c, i):
            x.wait()

        def strip(j, _):
            s = pl.ds(pl.multiple_of(c * count + i * piece + j * 16, 16), 16)
            total = bufs[0][s]
            for a in bufs[1:]:
                total = total + a[s].astype(jnp.float32)
            bufs[0][s] = total * factor
            return 0

        lax.fori_loop(0, piece // 16, strip, 0)
        copy_out(c, i).start()

    for body in (start, work, lambda c, i: copy_out(c, i).wait()):
        for c in range(len(chunks)):
            run(c, body)


def divided(weight, halved, chunks, arrived, out=None):
    n_rows, width = halved.shape
    count = n_rows // CHUNKS
    pieces = 4
    n_arrived = len(arrived[0])
    operands = [halved] + [x for messages in arrived for x in messages]
    aliases = {}
    if out is not None:
        operands.append(out)
        aliases = {len(operands): 0}
    anywhere = pl.BlockSpec(memory_space=pl.ANY)
    return pl.pallas_call(
        partial(sum_kernel, chunks, n_arrived),
        grid_spec=pltpu.PrefetchScalarGridSpec(
            num_scalar_prefetch=1,
            grid=(),
            in_specs=[anywhere] * len(operands),
            out_specs=anywhere,
            scratch_shapes=[pltpu.VMEM((len(chunks) * count, width), jnp.float32)]
            + [pltpu.VMEM((len(chunks) * count, width), jnp.bfloat16)] * n_arrived
            + [
                pltpu.SemaphoreType.DMA((len(chunks), 1 + n_arrived, pieces)),
                pltpu.SemaphoreType.DMA((len(chunks), pieces)),
            ],
        ),
        out_shape=jax.ShapeDtypeStruct((n_rows, width), jnp.float32),
        input_output_aliases=aliases,
        compiler_params=pltpu.CompilerParams(vmem_limit_bytes=VMEM),
        name="last_sum",
    )(weight, *operands)


def along(block, distance):
    n = lax.axis_size("gossip")
    return lax.ppermute(block, "gossip", [(i, i - i % RING + (i + distance) % RING) for i in range(n)])


def across(block, wrapped):
    n = lax.axis_size("gossip")
    return lax.ppermute(block, "gossip", [(i, (i + RING) % n if i % RING in wrapped else i) for i in range(n)])


def back_across(block, distance):
    n = lax.axis_size("gossip")
    to = [i - i % RING + (i - 1) % RING for i in range(n)]
    return lax.ppermute(block, "gossip", [(i, (t + RING) % n if t % RING < distance else t) for i, t in enumerate(to)])


def finish(near, far, weight, halved, m_near, m_far):
    if near == far:
        arrived = [pushed(m, 1 << near) for m in m_near]
        out = divided(weight, halved, (0,), [arrived[:1]])
        return divided(weight, halved, (1,), [arrived[1:]], out)
    first, second = exchange(near, far, m_near, m_far)
    return divided(weight, halved, (0, 1), list(zip(first, second)))


def exchange(k0, k1, m0, m1):
    crowded = max(1 << k0, 1 << k1) < RING
    begun = []
    for k, m in ((k0, m0), (k1, m1)):
        d = 1 << k
        if d >= RING:
            begun.append([pushed(x, d) for x in m])
        elif crowded and 2 * d == RING:
            begun.append([along(m[0], -1), m[1]])
        else:
            begun.append([along(m[0], d), across(m[1], range(RING - d, RING))])
    sent = []
    for k, m in zip((k0, k1), begun):
        d = 1 << k
        if d >= RING:
            sent.append(m)
        elif crowded and 2 * d == RING:
            sent.append([back_across(m[0], d), pushed(after(m[1], begun[0][0]), d)])
        else:
            sent.append([across(m[0], range(d)), along(m[1], d)])
    return sent[0], sent[1]


def per_device(numerator, push_weight, hidden_in, targets, exponents):
    numerators = numerator[0]
    n_rows, width = numerators.shape
    weight = push_weight.astype(jnp.float32)
    order = exponents
    f = lax.axis_index("fsdp").astype(jnp.int32)[None]

    n_tok = hidden_in.shape[2]
    mine0 = first_message(f, hidden_in, targets)
    chip0 = swap(mine0, 2)
    own0 = lax.slice(mine0, (0, 0), (n_tok, width))
    core0 = swap(own0, 1)
    t_core = swap(for_other_core(after(f, mine0), targets, n_rows), 1)
    own1 = normalized(after(hidden_in, mine0), 1)
    chip1 = swap(own1, 2)
    core1 = swap(own1, 1)
    current0 = after(numerators, own1).astype(jnp.bfloat16)
    step = partial(pair, weight=weight, order=order, f=f, n_tok=n_tok)
    [rows0] = step(0, False, left=[current0], ns=[own0, core0], ts=[targets, t_core], rows=numerators)

    received = []
    tile = after(jnp.broadcast_to(push_weight, (16, 128)), rows0)
    for k in range(EXPONENTS):
        tile = after(tile, *received)
        received.append(pushed(tile, 1 << k))
    received = [x[0, :1].astype(jnp.float32) for x in received]

    def chosen(k):
        return jnp.where(k == 0, received[0], jnp.where(k == 1, received[1], received[2]))

    weight_out = (weight * 0.25 + chosen(order[0]) * 0.5) + chosen(order[1]) * 0.25

    chip0 = after(chip0, weight_out)
    far0 = [chip0, swap(chip0, 1)]
    halved0, *m0 = step(0, True, left=[current0], ns=far0, ts=far0, rows=rows0)
    [rows1] = step(1, False, left=m0, ns=[own1, core1], ts=[targets, t_core], rows=halved0)
    chip1 = after(chip1, rows1)
    halved1, a0, a1, b0, b1 = step(1, True, left=m0, ns=[chip1, swap(chip1, 1)], ts=far0, rows=rows1)

    cases = [(near, far) for far in range(EXPONENTS) for near in range(far + 1)]
    near, far = jnp.minimum(order[0], order[1]), jnp.maximum(order[0], order[1])
    params = lax.switch(
        far * (far + 1) // 2 + near, [partial(finish, *c) for c in cases], weight_out, halved1, [a0, a1], [b0, b1]
    )
    return params[None], weight_out


def solution(mesh):
    in_specs = (
        P("gossip", "fsdp", None),
        P("gossip"),
        P(None, "gossip", "fsdp", None),
        P(None, "gossip", "fsdp", None),
        P(),
    )
    out_specs = (P("gossip", "fsdp", None), P("gossip"))
    return jax.shard_map(
        per_device, mesh=mesh, in_specs=in_specs, out_specs=out_specs, check_vma=False
    )
```

```python
from functools import partial
import math

import jax
import jax.numpy as jnp
from jax import lax
from jax.experimental import pallas as pl
from jax.experimental.pallas import tpu as pltpu
from jax.sharding import PartitionSpec as P

EXPONENTS = 3
CHUNKS = 2
RING = 4
TILE = 1024
VMEM = 63 * 2**20

learning_rate = 0.5
epsilon = 1e-06


def swap(block, bit):
    n = lax.axis_size("fsdp")
    return lax.ppermute(block, "fsdp", [(i, i ^ bit) for i in range(n)])


def pushed(block, distance):
    n = lax.axis_size("gossip")
    return lax.ppermute(block, "gossip", [(i, (i + distance) % n) for i in range(n)])


def after(block, *earlier):
    return lax.optimization_barrier((block, *earlier))[0]


def norm(h):
    values = h.astype(jnp.float32)
    scale = lax.rsqrt(jnp.mean(values * values, axis=-1, keepdims=True) + epsilon)
    return (values * scale).astype(jnp.bfloat16)


def norm_kernel(h_ref, out_ref):
    out_ref[...] = norm(h_ref[0, 0])


def normalized(hidden_in, step):
    _, _, n_tok, width = hidden_in.shape
    tile = 128
    return pl.pallas_call(
        norm_kernel,
        grid=(n_tok // tile,),
        in_specs=[pl.BlockSpec((1, 1, tile, width), lambda i: (step, 0, i, 0))],
        out_specs=pl.BlockSpec((tile, width), lambda i: (i, 0)),
        out_shape=jax.ShapeDtypeStruct((n_tok, width), jnp.bfloat16),
        compiler_params=pltpu.CompilerParams(vmem_limit_bytes=VMEM),
        name="normalize",
    )(hidden_in)


def first_kernel(f_ref, h_ref, t0_ref, t1_ref, out_ref):
    step = pl.program_id(0)

    @pl.when(step == 0)
    def _():
        out_ref[...] = norm(h_ref[0, 0])

    @pl.when(step == 1)
    def _():
        half = out_ref.shape[1] // 2
        out_ref[:, :half] = t0_ref[0, 0]
        out_ref[:, half:] = t1_ref[0, 0]


def first_message(f, hidden_in, targets):
    _, _, n_tok, width = hidden_in.shape
    half = width // 2
    tile = n_tok
    per_step = n_tok // tile

    def of_step(step):
        return pl.BlockSpec(
            (1, 1, tile, half), lambda part, i, f: (step, 0, i * part, jnp.bitwise_xor(f[0] // 2, 1))
        )

    return pl.pallas_call(
        first_kernel,
        grid_spec=pltpu.PrefetchScalarGridSpec(
            num_scalar_prefetch=1,
            grid=(2, per_step),
            in_specs=[
                pl.BlockSpec((1, 1, tile, width), lambda part, i, f: (0, 0, i * (1 - part) + (per_step - 1) * part, 0)),
                of_step(0),
                of_step(1),
            ],
            out_specs=pl.BlockSpec((tile, width), lambda part, i, f: (part * per_step + i, 0)),
        ),
        out_shape=jax.ShapeDtypeStruct((2 * n_tok, width), jnp.bfloat16),
        compiler_params=pltpu.CompilerParams(vmem_limit_bytes=VMEM),
        name="first_message",
    )(f, hidden_in, targets, targets)


def copy_kernel(f_ref, t_ref, out_ref):
    out_ref[0] = t_ref[0, 0]


def for_other_core(f, targets, n_rows):
    steps, _, n_tok, _ = targets.shape
    return pl.pallas_call(
        copy_kernel,
        grid_spec=pltpu.PrefetchScalarGridSpec(
            num_scalar_prefetch=1,
            grid=(steps,),
            in_specs=[pl.BlockSpec((1, 1, n_tok, n_rows), lambda s, f: (s, 0, 0, jnp.bitwise_xor(f[0], 1)))],
            out_specs=pl.BlockSpec((1, n_tok, n_rows), lambda s, f: (s, 0, 0)),
        ),
        out_shape=jax.ShapeDtypeStruct((steps, n_tok, n_rows), jnp.bfloat16),
        compiler_params=pltpu.CompilerParams(vmem_limit_bytes=VMEM),
        name="pack_targets",
    )(f, targets)


def pair_kernel(last, w_ref, order_ref, f_ref, l0, l1, n0, n1, t0, t1, rows_ref, *refs, step):
    deltas = refs[-1]
    half, width = l0.shape
    root_width = math.sqrt(width)
    n_tok = n0.shape[0]

    @pl.when(pl.program_id(0) == 0)
    def _():
        scale = 2.0**step / (root_width * w_ref[0])
        for b, (n, t) in enumerate(((n0, t0), (n1, t1))):
            goals = t[...].reshape(t.shape[-2:])
            for c, left in enumerate((l0, l1)):
                pre = scale * lax.dot_general(
                    n[...], left[...], (((1,), (1,)), ((), ())), preferred_element_type=jnp.float32
                )
                goal = goals[:, c * half : (c + 1) * half].astype(jnp.float32)
                sigma = jax.nn.sigmoid(pre)
                slope = sigma * (1.0 + pre * (1.0 - sigma))
                delta = ((pre * sigma - goal) * slope).astype(jnp.bfloat16)
                deltas[c * half : (c + 1) * half, b * n_tok : (b + 1) * n_tok] = delta.T

    k = pl.ds(pl.multiple_of(pl.program_id(0) * TILE, TILE), TILE)
    total = jnp.dot(deltas[:, :n_tok], n0[:, k], preferred_element_type=jnp.float32)
    total += jnp.dot(deltas[:, n_tok:], n1[:, k], preferred_element_type=jnp.float32)
    rows = rows_ref[...] - (learning_rate / root_width) * total
    if not last:
        refs[0][...] = rows
        return
    halved = rows * 0.5
    refs[0][...] = halved
    for c, left in enumerate((l0, l1)):
        here = halved[c * half : (c + 1) * half]
        message = here.astype(jnp.bfloat16)
        if step == 0:
            refs[1 + c][...] = message
        else:
            earlier = left[:, k]
            both = (earlier.astype(jnp.float32) + here).astype(jnp.bfloat16)
            swapped = order_ref[0] > order_ref[1]
            near = jnp.where(swapped, message, earlier)
            refs[1 + c][...] = jnp.where(order_ref[0] == order_ref[1], both, near)
            refs[3 + c][...] = jnp.where(swapped, earlier, message)


def pair(step, last, weight, order, f, n_tok, left, ns, ts, rows):
    n_rows, width = rows.shape
    half = n_rows // CHUNKS

    def goal(t):
        if t.ndim == 4:
            return pl.BlockSpec((1, 1, n_tok, n_rows), lambda j, w, s, f: (step, 0, 0, f[0]))
        if t.ndim == 3:
            return pl.BlockSpec((1, n_tok, n_rows), lambda j, w, s, f: (step, 0, 0))
        return pl.BlockSpec((n_tok, n_rows), lambda j, w, s, f: (1, step * 2 + f[0] % 2))

    if len(left) == 1:
        left = [left[0], left[0]]
        halves = [pl.BlockSpec((half, width), lambda j, w, s, f, c=c: (c, 0)) for c in range(CHUNKS)]
    else:
        halves = [pl.BlockSpec((half, width), lambda j, w, s, f: (0, 0))] * CHUNKS
    tile = pl.BlockSpec((n_rows, TILE), lambda j, w, s, f: (0, j))
    out_specs = [tile]
    out_shape = [jax.ShapeDtypeStruct((n_rows, width), jnp.float32)]
    if last:
        out_specs += [pl.BlockSpec((half, TILE), lambda j, w, s, f: (0, j))] * (2 + 2 * step)
        out_shape += [jax.ShapeDtypeStruct((half, width), jnp.bfloat16)] * (2 + 2 * step)
    return pl.pallas_call(
        partial(pair_kernel, last, step=step),
        grid_spec=pltpu.PrefetchScalarGridSpec(
            num_scalar_prefetch=3,
            grid=(width // TILE,),
            in_specs=halves
            + [pl.BlockSpec((n_tok, width), lambda j, w, s, f: (0, 0))] * 2
            + [goal(t) for t in ts]
            + [tile],
            out_specs=out_specs,
            scratch_shapes=[pltpu.VMEM((n_rows, 2 * n_tok), jnp.bfloat16)],
        ),
        out_shape=out_shape,
        compiler_params=pltpu.CompilerParams(vmem_limit_bytes=VMEM),
        cost_estimate=pl.CostEstimate(flops=2**20, bytes_accessed=2**20, transcendentals=0),
        name="pair_of_blocks",
    )(weight, order, f, *left, *ns, *ts, rows)


def sum_kernel(chunks, n_arrived, w_ref, *refs):
    source, arrived = refs[0], refs[1 : 1 + len(chunks) * n_arrived]
    out = refs[-(n_arrived + 4)]
    bufs, (in_sems, out_sems) = refs[-(n_arrived + 3) : -2], refs[-2:]
    pieces = in_sems.shape[2]
    count = bufs[0].shape[0] // len(chunks)
    piece = count // pieces
    factor = 1.0 / w_ref[0]

    def rows(at, i):
        return pl.ds(pl.multiple_of(at * count + i * piece, piece), piece)

    def copies_in(c, i):
        froms = [source.at[rows(chunks[c], i)]]
        froms += [a.at[rows(0, i)] for a in arrived[c * n_arrived : (c + 1) * n_arrived]]
        return [
            pltpu.make_async_copy(x, bufs[a].at[rows(c, i)], in_sems.at[c, a, i]) for a, x in enumerate(froms)
        ]

    def copy_out(c, i):
        return pltpu.make_async_copy(bufs[0].at[rows(c, i)], out.at[rows(chunks[c], i)], out_sems.at[c, i])

    def run(c, body):
        lax.fori_loop(0, pieces, lambda i, _: (body(c, i), 0)[1], 0)

    def start(c, i):
        for x in copies_in(c, i):
            x.start()

    def work(c, i):
        for x in copies_in(c, i):
            x.wait()

        def strip(j, _):
            s = pl.ds(pl.multiple_of(c * count + i * piece + j * 16, 16), 16)
            total = bufs[0][s]
            for a in bufs[1:]:
                total = total + a[s].astype(jnp.float32)
            bufs[0][s] = total * factor
            return 0

        lax.fori_loop(0, piece // 16, strip, 0)
        copy_out(c, i).start()

    for body in (start, work, lambda c, i: copy_out(c, i).wait()):
        for c in range(len(chunks)):
            run(c, body)


def divided(weight, halved, chunks, arrived, out=None):
    n_rows, width = halved.shape
    count = n_rows // CHUNKS
    pieces = 4
    n_arrived = len(arrived[0])
    operands = [halved] + [x for messages in arrived for x in messages]
    aliases = {}
    if out is not None:
        operands.append(out)
        aliases = {len(operands): 0}
    anywhere = pl.BlockSpec(memory_space=pl.ANY)
    return pl.pallas_call(
        partial(sum_kernel, chunks, n_arrived),
        grid_spec=pltpu.PrefetchScalarGridSpec(
            num_scalar_prefetch=1,
            grid=(),
            in_specs=[anywhere] * len(operands),
            out_specs=anywhere,
            scratch_shapes=[pltpu.VMEM((len(chunks) * count, width), jnp.float32)]
            + [pltpu.VMEM((len(chunks) * count, width), jnp.bfloat16)] * n_arrived
            + [
                pltpu.SemaphoreType.DMA((len(chunks), 1 + n_arrived, pieces)),
                pltpu.SemaphoreType.DMA((len(chunks), pieces)),
            ],
        ),
        out_shape=jax.ShapeDtypeStruct((n_rows, width), jnp.float32),
        input_output_aliases=aliases,
        compiler_params=pltpu.CompilerParams(vmem_limit_bytes=VMEM),
        name="last_sum",
    )(weight, *operands)


def along(block, distance):
    n = lax.axis_size("gossip")
    return lax.ppermute(block, "gossip", [(i, i - i % RING + (i + distance) % RING) for i in range(n)])


def across(block, wrapped):
    n = lax.axis_size("gossip")
    return lax.ppermute(block, "gossip", [(i, (i + RING) % n if i % RING in wrapped else i) for i in range(n)])


def back_across(block, distance):
    n = lax.axis_size("gossip")
    to = [i - i % RING + (i - 1) % RING for i in range(n)]
    return lax.ppermute(
        block, "gossip", [(i, (t + RING) % n if i % RING >= RING - distance else t) for i, t in enumerate(to)]
    )


def finish(near, far, weight, halved, m_near, m_far):
    if near == far:
        arrived = [pushed(m, 1 << near) for m in m_near]
        out = divided(weight, halved, (0,), [arrived[:1]])
        return divided(weight, halved, (1,), [arrived[1:]], out)
    first, second = exchange(near, far, m_near, m_far)
    return divided(weight, halved, (0, 1), list(zip(first, second)))


def exchange(k0, k1, m0, m1):
    crowded = max(1 << k0, 1 << k1) < RING
    begun = []
    for k, m in ((k0, m0), (k1, m1)):
        d = 1 << k
        if d >= RING:
            begun.append([pushed(x, d) for x in m])
        elif crowded and 2 * d == RING:
            begun.append([back_across(m[0], d), m[1]])
        else:
            begun.append([along(m[0], d), across(m[1], range(RING - d, RING))])
    sent = []
    for k, m in zip((k0, k1), begun):
        d = 1 << k
        if d >= RING:
            sent.append(m)
        elif crowded and 2 * d == RING:
            sent.append([along(m[0], -1), pushed(after(m[1], begun[0][0]), d)])
        else:
            sent.append([across(m[0], range(d)), along(m[1], d)])
    return sent[0], sent[1]


def per_device(numerator, push_weight, hidden_in, targets, exponents):
    numerators = numerator[0]
    n_rows, width = numerators.shape
    weight = push_weight.astype(jnp.float32)
    order = exponents
    f = lax.axis_index("fsdp").astype(jnp.int32)[None]

    n_tok = hidden_in.shape[2]
    mine0 = first_message(f, hidden_in, targets)
    chip0 = swap(mine0, 2)
    own0 = lax.slice(mine0, (0, 0), (n_tok, width))
    core0 = swap(own0, 1)
    t_core = swap(for_other_core(after(f, mine0), targets, n_rows), 1)
    own1 = normalized(after(hidden_in, mine0), 1)
    chip1 = swap(own1, 2)
    core1 = swap(own1, 1)
    current0 = after(numerators, own1).astype(jnp.bfloat16)
    step = partial(pair, weight=weight, order=order, f=f, n_tok=n_tok)
    [rows0] = step(0, False, left=[current0], ns=[own0, core0], ts=[targets, t_core], rows=numerators)

    received = []
    tile = after(jnp.broadcast_to(push_weight, (16, 128)), rows0)
    for k in range(EXPONENTS):
        tile = after(tile, *received)
        received.append(pushed(tile, 1 << k))
    received = [x[0, :1].astype(jnp.float32) for x in received]

    def chosen(k):
        return jnp.where(k == 0, received[0], jnp.where(k == 1, received[1], received[2]))

    weight_out = (weight * 0.25 + chosen(order[0]) * 0.5) + chosen(order[1]) * 0.25

    chip0 = after(chip0, weight_out)
    far0 = [chip0, swap(chip0, 1)]
    halved0, *m0 = step(0, True, left=[current0], ns=far0, ts=far0, rows=rows0)
    [rows1] = step(1, False, left=m0, ns=[own1, core1], ts=[targets, t_core], rows=halved0)
    chip1 = after(chip1, rows1)
    halved1, a0, a1, b0, b1 = step(1, True, left=m0, ns=[chip1, swap(chip1, 1)], ts=far0, rows=rows1)

    cases = [(near, far) for far in range(EXPONENTS) for near in range(far + 1)]
    near, far = jnp.minimum(order[0], order[1]), jnp.maximum(order[0], order[1])
    params = lax.switch(
        far * (far + 1) // 2 + near, [partial(finish, *c) for c in cases], weight_out, halved1, [a0, a1], [b0, b1]
    )
    return params[None], weight_out


def solution(mesh):
    in_specs = (
        P("gossip", "fsdp", None),
        P("gossip"),
        P(None, "gossip", "fsdp", None),
        P(None, "gossip", "fsdp", None),
        P(),
    )
    out_specs = (P("gossip", "fsdp", None), P("gossip"))
    return jax.shard_map(
        per_device, mesh=mesh, in_specs=in_specs, out_specs=out_specs, check_vma=False
    )
```

```python
from functools import partial
import math

import jax
import jax.numpy as jnp
from jax import lax
from jax.experimental import pallas as pl
from jax.experimental.pallas import tpu as pltpu
from jax.sharding import PartitionSpec as P

EXPONENTS = 3
CHUNKS = 2
RING = 4
TILE = 1024
VMEM = 36 * 2**20
ALL_VMEM = 63 * 2**20

learning_rate = 0.5
epsilon = 1e-06


def swap(block, bit):
    n = lax.axis_size("fsdp")
    return lax.ppermute(block, "fsdp", [(i, i ^ bit) for i in range(n)])


def pushed(block, distance):
    n = lax.axis_size("gossip")
    return lax.ppermute(block, "gossip", [(i, (i + distance) % n) for i in range(n)])


def after(block, *earlier):
    return lax.optimization_barrier((block, *earlier))[0]


def norm(h):
    values = h.astype(jnp.float32)
    scale = lax.rsqrt(jnp.mean(values * values, axis=-1, keepdims=True) + epsilon)
    return (values * scale).astype(jnp.bfloat16)


def norm_kernel(h_ref, out_ref):
    out_ref[...] = norm(h_ref[0, 0])


def normalized(hidden_in, step):
    _, _, n_tok, width = hidden_in.shape
    tile = 128
    return pl.pallas_call(
        norm_kernel,
        grid=(n_tok // tile,),
        in_specs=[pl.BlockSpec((1, 1, tile, width), lambda i: (step, 0, i, 0))],
        out_specs=pl.BlockSpec((tile, width), lambda i: (i, 0)),
        out_shape=jax.ShapeDtypeStruct((n_tok, width), jnp.bfloat16),
        compiler_params=pltpu.CompilerParams(vmem_limit_bytes=VMEM),
        name="normalize",
    )(hidden_in)


def first_kernel(f_ref, h_ref, t0_ref, t1_ref, out_ref):
    step = pl.program_id(0)

    @pl.when(step == 0)
    def _():
        out_ref[...] = norm(h_ref[0, 0])

    @pl.when(step == 1)
    def _():
        half = out_ref.shape[1] // 2
        out_ref[:, :half] = t0_ref[0, 0]
        out_ref[:, half:] = t1_ref[0, 0]


def first_message(f, hidden_in, targets):
    _, _, n_tok, width = hidden_in.shape
    half = width // 2
    tile = n_tok
    per_step = n_tok // tile

    def of_step(step):
        return pl.BlockSpec(
            (1, 1, tile, half), lambda part, i, f: (step, 0, i * part, jnp.bitwise_xor(f[0] // 2, 1))
        )

    return pl.pallas_call(
        first_kernel,
        grid_spec=pltpu.PrefetchScalarGridSpec(
            num_scalar_prefetch=1,
            grid=(2, per_step),
            in_specs=[
                pl.BlockSpec((1, 1, tile, width), lambda part, i, f: (0, 0, i * (1 - part) + (per_step - 1) * part, 0)),
                of_step(0),
                of_step(1),
            ],
            out_specs=pl.BlockSpec((tile, width), lambda part, i, f: (part * per_step + i, 0)),
        ),
        out_shape=jax.ShapeDtypeStruct((2 * n_tok, width), jnp.bfloat16),
        compiler_params=pltpu.CompilerParams(vmem_limit_bytes=VMEM),
        name="first_message",
    )(f, hidden_in, targets, targets)


def copy_kernel(f_ref, t_ref, out_ref):
    out_ref[0] = t_ref[0, 0]


def for_other_core(f, targets, n_rows):
    steps, _, n_tok, _ = targets.shape
    return pl.pallas_call(
        copy_kernel,
        grid_spec=pltpu.PrefetchScalarGridSpec(
            num_scalar_prefetch=1,
            grid=(steps,),
            in_specs=[pl.BlockSpec((1, 1, n_tok, n_rows), lambda s, f: (s, 0, 0, jnp.bitwise_xor(f[0], 1)))],
            out_specs=pl.BlockSpec((1, n_tok, n_rows), lambda s, f: (s, 0, 0)),
        ),
        out_shape=jax.ShapeDtypeStruct((steps, n_tok, n_rows), jnp.bfloat16),
        compiler_params=pltpu.CompilerParams(vmem_limit_bytes=VMEM),
        name="pack_targets",
    )(f, targets)


def pair_kernel(last, w_ref, order_ref, f_ref, l0, l1, n0, n1, t0, t1, rows_ref, *refs, step):
    deltas = refs[-1]
    half, width = l0.shape
    root_width = math.sqrt(width)
    n_tok = n0.shape[0]

    @pl.when(pl.program_id(0) == 0)
    def _():
        scale = 2.0**step / (root_width * w_ref[0])
        for b, (n, t) in enumerate(((n0, t0), (n1, t1))):
            goals = t[...].reshape(t.shape[-2:])
            for c, left in enumerate((l0, l1)):
                pre = scale * lax.dot_general(
                    n[...], left[...], (((1,), (1,)), ((), ())), preferred_element_type=jnp.float32
                )
                goal = goals[:, c * half : (c + 1) * half].astype(jnp.float32)
                sigma = jax.nn.sigmoid(pre)
                slope = sigma * (1.0 + pre * (1.0 - sigma))
                delta = ((pre * sigma - goal) * slope).astype(jnp.bfloat16)
                deltas[c * half : (c + 1) * half, b * n_tok : (b + 1) * n_tok] = delta.T

    k = pl.ds(pl.multiple_of(pl.program_id(0) * TILE, TILE), TILE)
    total = jnp.dot(deltas[:, :n_tok], n0[:, k], preferred_element_type=jnp.float32)
    total += jnp.dot(deltas[:, n_tok:], n1[:, k], preferred_element_type=jnp.float32)
    rows = rows_ref[...] - (learning_rate / root_width) * total
    if not last:
        refs[0][...] = rows
        return
    halved = rows * 0.5
    refs[0][...] = halved
    for c, left in enumerate((l0, l1)):
        here = halved[c * half : (c + 1) * half]
        message = here.astype(jnp.bfloat16)
        if step == 0:
            refs[1 + c][...] = message
        else:
            earlier = left[:, k]
            both = (earlier.astype(jnp.float32) + here).astype(jnp.bfloat16)
            swapped = order_ref[0] > order_ref[1]
            near = jnp.where(swapped, message, earlier)
            refs[1 + c][...] = jnp.where(order_ref[0] == order_ref[1], both, near)
            refs[3 + c][...] = jnp.where(swapped, earlier, message)


def pair(step, last, weight, order, f, n_tok, left, ns, ts, rows):
    n_rows, width = rows.shape
    half = n_rows // CHUNKS

    def goal(t):
        if t.ndim == 4:
            return pl.BlockSpec((1, 1, n_tok, n_rows), lambda j, w, s, f: (step, 0, 0, f[0]))
        if t.ndim == 3:
            return pl.BlockSpec((1, n_tok, n_rows), lambda j, w, s, f: (step, 0, 0))
        return pl.BlockSpec((n_tok, n_rows), lambda j, w, s, f: (1, step * 2 + f[0] % 2))

    if len(left) == 1:
        left = [left[0], left[0]]
        halves = [pl.BlockSpec((half, width), lambda j, w, s, f, c=c: (c, 0)) for c in range(CHUNKS)]
    else:
        halves = [pl.BlockSpec((half, width), lambda j, w, s, f: (0, 0))] * CHUNKS
    tile = pl.BlockSpec((n_rows, TILE), lambda j, w, s, f: (0, j))
    out_specs = [tile]
    out_shape = [jax.ShapeDtypeStruct((n_rows, width), jnp.float32)]
    if last:
        out_specs += [pl.BlockSpec((half, TILE), lambda j, w, s, f: (0, j))] * (2 + 2 * step)
        out_shape += [jax.ShapeDtypeStruct((half, width), jnp.bfloat16)] * (2 + 2 * step)
    return pl.pallas_call(
        partial(pair_kernel, last, step=step),
        grid_spec=pltpu.PrefetchScalarGridSpec(
            num_scalar_prefetch=3,
            grid=(width // TILE,),
            in_specs=halves
            + [pl.BlockSpec((n_tok, width), lambda j, w, s, f: (0, 0))] * 2
            + [goal(t) for t in ts]
            + [tile],
            out_specs=out_specs,
            scratch_shapes=[pltpu.VMEM((n_rows, 2 * n_tok), jnp.bfloat16)],
        ),
        out_shape=out_shape,
        compiler_params=pltpu.CompilerParams(vmem_limit_bytes=ALL_VMEM if last and step else VMEM),
        cost_estimate=pl.CostEstimate(flops=2**20, bytes_accessed=2**20, transcendentals=0),
        name="pair_of_blocks",
    )(weight, order, f, *left, *ns, *ts, rows)


def sum_kernel(chunks, n_arrived, w_ref, *refs):
    source, arrived = refs[0], refs[1 : 1 + len(chunks) * n_arrived]
    out = refs[-(n_arrived + 4)]
    bufs, (in_sems, out_sems) = refs[-(n_arrived + 3) : -2], refs[-2:]
    pieces = in_sems.shape[2]
    count = bufs[0].shape[0] // len(chunks)
    piece = count // pieces
    factor = 1.0 / w_ref[0]

    def rows(at, i):
        return pl.ds(pl.multiple_of(at * count + i * piece, piece), piece)

    def copies_in(c, i):
        froms = [source.at[rows(chunks[c], i)]]
        froms += [a.at[rows(0, i)] for a in arrived[c * n_arrived : (c + 1) * n_arrived]]
        return [
            pltpu.make_async_copy(x, bufs[a].at[rows(c, i)], in_sems.at[c, a, i]) for a, x in enumerate(froms)
        ]

    def copy_out(c, i):
        return pltpu.make_async_copy(bufs[0].at[rows(c, i)], out.at[rows(chunks[c], i)], out_sems.at[c, i])

    def run(c, body):
        lax.fori_loop(0, pieces, lambda i, _: (body(c, i), 0)[1], 0)

    def start(c, i):
        for x in copies_in(c, i):
            x.start()

    def work(c, i):
        for x in copies_in(c, i):
            x.wait()

        def strip(j, _):
            s = pl.ds(pl.multiple_of(c * count + i * piece + j * 16, 16), 16)
            total = bufs[0][s]
            for a in bufs[1:]:
                total = total + a[s].astype(jnp.float32)
            bufs[0][s] = total * factor
            return 0

        lax.fori_loop(0, piece // 16, strip, 0)
        copy_out(c, i).start()

    for body in (start, work, lambda c, i: copy_out(c, i).wait()):
        for c in range(len(chunks)):
            run(c, body)


def divided(weight, halved, chunks, arrived, out=None):
    n_rows, width = halved.shape
    count = n_rows // CHUNKS
    pieces = 4
    n_arrived = len(arrived[0])
    operands = [halved] + [x for messages in arrived for x in messages]
    aliases = {}
    if out is not None:
        operands.append(out)
        aliases = {len(operands): 0}
    anywhere = pl.BlockSpec(memory_space=pl.ANY)
    return pl.pallas_call(
        partial(sum_kernel, chunks, n_arrived),
        grid_spec=pltpu.PrefetchScalarGridSpec(
            num_scalar_prefetch=1,
            grid=(),
            in_specs=[anywhere] * len(operands),
            out_specs=anywhere,
            scratch_shapes=[pltpu.VMEM((len(chunks) * count, width), jnp.float32)]
            + [pltpu.VMEM((len(chunks) * count, width), jnp.bfloat16)] * n_arrived
            + [
                pltpu.SemaphoreType.DMA((len(chunks), 1 + n_arrived, pieces)),
                pltpu.SemaphoreType.DMA((len(chunks), pieces)),
            ],
        ),
        out_shape=jax.ShapeDtypeStruct((n_rows, width), jnp.float32),
        input_output_aliases=aliases,
        compiler_params=pltpu.CompilerParams(vmem_limit_bytes=ALL_VMEM),
        name="last_sum",
    )(weight, *operands)


def along(block, distance):
    n = lax.axis_size("gossip")
    return lax.ppermute(block, "gossip", [(i, i - i % RING + (i + distance) % RING) for i in range(n)])


def across(block, wrapped):
    n = lax.axis_size("gossip")
    return lax.ppermute(block, "gossip", [(i, (i + RING) % n if i % RING in wrapped else i) for i in range(n)])


def back_across(block, distance):
    n = lax.axis_size("gossip")
    to = [i - i % RING + (i - 1) % RING for i in range(n)]
    return lax.ppermute(
        block, "gossip", [(i, (t + RING) % n if i % RING >= RING - distance else t) for i, t in enumerate(to)]
    )


def finish(near, far, weight, halved, m_near, m_far):
    if near == far:
        arrived = [pushed(m, 1 << near) for m in m_near]
        out = divided(weight, halved, (0,), [arrived[:1]])
        return divided(weight, halved, (1,), [arrived[1:]], out)
    first, second = exchange(near, far, m_near, m_far)
    return divided(weight, halved, (0, 1), list(zip(first, second)))


def exchange(k0, k1, m0, m1):
    crowded = max(1 << k0, 1 << k1) < RING
    begun = []
    for k, m in ((k0, m0), (k1, m1)):
        d = 1 << k
        if d >= RING:
            begun.append([pushed(x, d) for x in m])
        elif crowded and 2 * d == RING:
            begun.append([back_across(m[0], d), m[1]])
        else:
            begun.append([along(m[0], d), across(m[1], range(RING - d, RING))])
    sent = []
    for k, m in zip((k0, k1), begun):
        d = 1 << k
        if d >= RING:
            sent.append(m)
        elif crowded and 2 * d == RING:
            sent.append([along(m[0], -1), pushed(after(m[1], begun[0][0]), d)])
        else:
            sent.append([across(m[0], range(d)), along(m[1], d)])
    return sent[0], sent[1]


def per_device(numerator, push_weight, hidden_in, targets, exponents):
    numerators = numerator[0]
    n_rows, width = numerators.shape
    weight = push_weight.astype(jnp.float32)
    order = exponents
    f = lax.axis_index("fsdp").astype(jnp.int32)[None]

    n_tok = hidden_in.shape[2]
    mine0 = first_message(f, hidden_in, targets)
    chip0 = swap(mine0, 2)
    own0 = lax.slice(mine0, (0, 0), (n_tok, width))
    core0 = swap(own0, 1)
    t_core = swap(for_other_core(after(f, mine0), targets, n_rows), 1)
    own1 = normalized(after(hidden_in, mine0), 1)
    chip1 = swap(own1, 2)
    core1 = swap(own1, 1)
    current0 = after(numerators, own1).astype(jnp.bfloat16)
    step = partial(pair, weight=weight, order=order, f=f, n_tok=n_tok)
    [rows0] = step(0, False, left=[current0], ns=[own0, core0], ts=[targets, t_core], rows=numerators)

    received = []
    tile = after(jnp.broadcast_to(push_weight, (16, 128)), rows0)
    for k in range(EXPONENTS):
        tile = after(tile, *received)
        received.append(pushed(tile, 1 << k))
    received = [x[0, :1].astype(jnp.float32) for x in received]

    def chosen(k):
        return jnp.where(k == 0, received[0], jnp.where(k == 1, received[1], received[2]))

    weight_out = (weight * 0.25 + chosen(order[0]) * 0.5) + chosen(order[1]) * 0.25

    chip0 = after(chip0, weight_out)
    far0 = [chip0, swap(chip0, 1)]
    halved0, *m0 = step(0, True, left=[current0], ns=far0, ts=far0, rows=rows0)
    [rows1] = step(1, False, left=m0, ns=[own1, core1], ts=[targets, t_core], rows=halved0)
    chip1 = after(chip1, rows1)
    halved1, a0, a1, b0, b1 = step(1, True, left=m0, ns=[chip1, swap(chip1, 1)], ts=far0, rows=rows1)

    cases = [(near, far) for far in range(EXPONENTS) for near in range(far + 1)]
    near, far = jnp.minimum(order[0], order[1]), jnp.maximum(order[0], order[1])
    params = lax.switch(
        far * (far + 1) // 2 + near, [partial(finish, *c) for c in cases], weight_out, halved1, [a0, a1], [b0, b1]
    )
    return params[None], weight_out


def solution(mesh):
    in_specs = (
        P("gossip", "fsdp", None),
        P("gossip"),
        P(None, "gossip", "fsdp", None),
        P(None, "gossip", "fsdp", None),
        P(),
    )
    out_specs = (P("gossip", "fsdp", None), P("gossip"))
    return jax.shard_map(
        per_device, mesh=mesh, in_specs=in_specs, out_specs=out_specs, check_vma=False
    )
```
